256 devices in a mesh: chain: 32 (over z_lo, y, core), tp: 8 (over z_hi, x).
Axes of the slice: x: 4, y: 4, z: 8 (z_hi: 2, z_lo: 4; z = z_hi * 4 + z_lo), core: 2. Of those that a mesh axis runs over, the one named last changes fastest.
Arguments:
- hidden_first: bfloat16 [28672, 8192], P('chain', 'tp')
- hidden_second: bfloat16 [28672, 8192], P('chain', 'tp')
- weight_buffer: bfloat16 [32, 2, 8192, 2048], P('chain', None, 'tp'), may hold values from -0.0625 to 0.0625
- gain_buffer: bfloat16 [32, 2, 8192], P('chain', None, 'tp'), may hold values from 0.25 to 1.75
- loaded_layers: int32 [32], P('chain'), may hold values from 0 to 2, as said below
- positions: int32 [28672], P('chain'), may hold values from 0 to 4542, as said below
Outputs:
- cache_rows: bfloat16 [2, 28672, 2048], P(None, 'chain', 'tp')
The draws below stay inside these ranges and needn't reach their ends.
Inputs may be any that keep to these rules, and one draw needn't show every extreme that they name: `loaded_layers`: entry 0, the source instance, holds all 2 layers. Each instance's rows are two prompts of 448 tokens; each prompt's positions are consecutive from its own start.
All inputs are finite; a program needn't handle non-finite values.
Results may differ from the reference program's by a relative error of at most 0.018.
Values may be sent and summed in bfloat16 or wider, within the bound.
No kernel may reach another device: no remote copies, remote signals or barrier semaphores. Data moves between devices by JAX's collectives and lax.ppermute only.
A program may use at most 128 MiB of HBM per device.

```python
import math
import jax
import jax.numpy as jnp
from jax import lax

D = 8192
KVH = 8
HD = 128
LAYERS = 2
TOK_INST = 896
TOKENS = 28672
N_CHAIN = 32
N_TP = 8


def column_rows(key, trend_base):
    key_rough, key_rows = jax.random.split(key, 2)
    col = jnp.arange(D, dtype=jnp.float32) / D
    rough = jnp.exp(jax.random.uniform(key_rough, (1, D), jnp.float32, -0.4, 0.4))
    trend = (trend_base ** (0.5 * col))[None, :]
    rows = jnp.exp(jax.random.uniform(key_rows, (TOKENS, 1), jnp.float32, 0.0, math.log(10.0)))
    return trend * rough * rows


def draw_hidden_first(key, part):
    key = jax.random.fold_in(key, 11)
    key_base, key_scale = jax.random.split(key, 2)
    base = jnp.clip(jax.random.normal(key_base, (TOKENS, D), jnp.float32), -5.0, 5.0)
    values = base * column_rows(key_scale, 3.0)
    return values.astype(jnp.bfloat16)


def draw_hidden_second(key, part):
    key = jax.random.fold_in(key, 23)
    key_base, key_scale = jax.random.split(key, 2)
    base = jnp.clip(jax.random.normal(key_base, (TOKENS, D), jnp.float32), -5.0, 5.0)
    values = base * column_rows(key_scale, 3.0)
    return values.astype(jnp.bfloat16)


def draw_loaded_layers(key, part):
    key = jax.random.fold_in(key, 37)
    counts = jax.random.randint(key, (N_CHAIN,), 0, LAYERS + 1)
    return counts.at[0].set(LAYERS).astype(jnp.int32)


def draw_positions(key, part):
    key = jax.random.fold_in(key, 41)
    key_starts, key_top, key_low = jax.random.split(key, 3)
    prompts = 2 * N_CHAIN
    starts = jax.random.randint(key_starts, (prompts,), 0, 4096)
    top_index = jax.random.randint(key_top, (), 0, prompts)
    low_index = (top_index + 1 + jax.random.randint(key_low, (), 0, prompts - 1)) % prompts
    starts = starts.at[top_index].set(4095)
    starts = starts.at[low_index].set(0)
    steps = jnp.arange(TOK_INST // 2, dtype=jnp.int32)[None, :]
    return (starts[:, None] + steps).reshape(TOKENS).astype(jnp.int32)


def steps_of(own_key, dims, shards, low, largest):
    def one(position, shards_of):
        heights = jax.random.uniform(jax.random.fold_in(jax.random.fold_in(own_key, 6), position), (shards_of,), jnp.float32, low / len(shards), largest / len(shards))
        return jnp.repeat(jnp.exp(heights), dims[position] // shards_of).reshape((-1,) + (1,) * (len(dims) - position - 1))

    level = one(*shards[0])
    for cut in shards[1:]:
        level = level * one(*cut)
    return level


def bell_draw(own_key, extent, scale, reach, cuts=(), kind=jnp.bfloat16):
    level = steps_of(own_key, extent, cuts, -0.22, 0.18) if cuts else 1.0
    array = jax.random.normal(own_key, extent, jnp.float32) * scale * level
    return jnp.minimum(jnp.maximum(array, -reach), reach).astype(kind)


def setup_inputs(seed: int = 0) -> dict:
    splits = jax.random.split(jax.random.key(seed), 7)
    return {
        "hidden_first": draw_hidden_first(jax.random.fold_in(splits[6], 71), 0),
        "hidden_second": draw_hidden_second(jax.random.fold_in(splits[6], 71), 0),
        "weight_buffer": bell_draw(splits[2], (N_CHAIN, LAYERS, D, KVH * 2 * HD), D ** -0.5, 0.0625, ((0, 32), (2, 8))),
        "gain_buffer": jnp.clip(1.0 + 0.15 * jax.random.normal(splits[3], (N_CHAIN, LAYERS, D), jnp.float32), 0.25, 1.75).astype(jnp.bfloat16),
        "loaded_layers": draw_loaded_layers(jax.random.fold_in(splits[6], 71), 0),
        "positions": draw_positions(jax.random.fold_in(splits[6], 71), 0),
    }


def rotate(keys, positions):
    half = keys.shape[-1] // 2
    freq = 500000.0 ** (-2.0 * jnp.arange(half, dtype=jnp.float32) / keys.shape[-1])
    angle = positions.astype(jnp.float32)[:, None] * freq[None, :]
    cosine = jnp.cos(angle)[:, None, :]
    sine = jnp.sin(angle)[:, None, :]
    first = keys[..., :half]
    second = keys[..., half:]
    return jnp.concatenate([first * cosine - second * sine, second * cosine + first * sine], axis=-1)

def project(rows, weights, gains, positions):
    count = rows.shape[0]
    wide = rows.astype(jnp.float32)
    meansq = lax.optimization_barrier(jnp.sum(wide * wide, axis=1)) / D
    scaled = (wide * gains.astype(jnp.float32)[None, :]).astype(jnp.bfloat16)
    blocks = scaled.reshape(count, N_TP, D // N_TP).astype(jnp.float32)
    wblocks = weights.reshape(N_TP, D // N_TP, KVH * 2 * HD).astype(jnp.float32)
    partial_value = jnp.einsum('tsd,sde->tse', blocks, wblocks).astype(jnp.bfloat16)
    summed = lax.optimization_barrier(jnp.sum(partial_value.astype(jnp.float32), axis=1))
    mixed = summed * lax.rsqrt(meansq + 1e-05)[:, None]
    heads = mixed.reshape(count, KVH, 2 * HD)
    keys = rotate(heads[..., :HD], positions)
    joined = jnp.concatenate([keys, heads[..., HD:]], axis=-1)
    return joined.reshape(count, KVH * 2 * HD).astype(jnp.bfloat16)

def reference(hidden_first, hidden_second, weight_buffer, gain_buffer, loaded_layers, positions):
    inputs = (hidden_first, hidden_second)
    results = []
    for layer in range(LAYERS):
        source_w = weight_buffer[0, layer]
        source_g = gain_buffer[0, layer]
        rows_all = inputs[layer].reshape(N_CHAIN, TOK_INST, D)
        pos_all = positions.reshape(N_CHAIN, TOK_INST)

        def one(index):
            resident = loaded_layers[index] > layer
            weights = jnp.where(resident, weight_buffer[index, layer], source_w)
            gains = jnp.where(resident, gain_buffer[index, layer], source_g)
            return project(rows_all[index], weights, gains, pos_all[index])
        rows_out = lax.map(one, jnp.arange(N_CHAIN, dtype=jnp.int32))
        results.append(rows_out.reshape(N_CHAIN * TOK_INST, KVH * 2 * HD))
    return jnp.stack(results, axis=0)
```

```python
import functools

import jax
import jax.numpy as jnp
from jax import lax
from jax.experimental import pallas as pl
from jax.experimental.pallas import tpu as pltpu
from jax.sharding import PartitionSpec as P

HD = 128
LAYERS = 2
NY, NX, NZ = 4, 4, 4
MIB = 1 << 20


def chain_pairs(step):
    pairs = []
    for z in range(NZ):
        for y in range(NY):
            for c in range(2):
                to = step(z, y, c)
                if to is not None:
                    z2, y2, c2 = to
                    pairs.append(((z * NY + y) * 2 + c, (z2 * NY + y2 % NY) * 2 + c2))
    return pairs


def tp_pairs(step):
    pairs = []
    for h in range(2):
        for x in range(NX):
            h2, x2 = step(h, x)
            pairs.append((h * NX + x, (h2 % 2) * NX + x2 % NX))
    return pairs


X_NEXT = tp_pairs(lambda h, x: (h, x + 1))
X_LAST = tp_pairs(lambda h, x: (h, x - 1))
H_SWAP = tp_pairs(lambda h, x: (h + 1, x))
Z_FAR = chain_pairs(lambda z, y, c: (2, y, 0) if (z, c) == (0, 0) else None)
Z_NEAR = chain_pairs(lambda z, y, c: (z + 1, y, 0) if z in (0, 2) and c == 0 else None)
CORE = chain_pairs(lambda z, y, c: (z, y, 1) if c == 0 else None)
ROWS = [[z * NY * 2 + k for k in range(NY * 2)] for z in range(NZ)]


def scatter_pairs(k):
    return chain_pairs(lambda z, y, c: (0, k, 0) if (z, y, c) == (0, 0, 0) else None)


def spread(weights, gains):
    me = lax.axis_index("chain")
    z, y, c = me // (2 * NY), me // 2 % NY, me % 2
    depth = weights.shape[0] // NY

    def piece(k):
        rows = weights[k * depth:(k + 1) * depth].astype(jnp.float32)
        return (rows * gains[k * depth:(k + 1) * depth, None].astype(jnp.float32)).astype(jnp.bfloat16)

    got = {k: lax.ppermute(piece(k), "chain", scatter_pairs(k)) for k in (2, 1, 3)}
    first = jnp.where(y == 0, piece(0), jnp.where(y == 1, got[1], jnp.where(y == 2, got[2], got[3])))
    far = lax.ppermute(first, "chain", Z_FAR)
    second = jnp.where(z == 2, far, first)
    near = lax.ppermute(second, "chain", Z_NEAR)
    mine = jnp.where((z == 1) | (z == 3), near, second)
    other = lax.ppermute(mine[depth // 2:], "chain", CORE)
    half = jnp.where(c == 0, mine[:depth // 2], other)
    return lax.all_gather(half, "chain", axis_index_groups=ROWS, axis=0, tiled=True)


def product_kernel(flags, x_ref, g_ref, own_ref, src_ref, out_ref, scaled):
    @pl.when(pl.program_id(0) == 0)
    def _():
        gain = jnp.where(flags[0] > 0, g_ref[...].astype(jnp.float32), 1.0)
        scaled[...] = (x_ref[...].astype(jnp.float32) * gain).astype(jnp.bfloat16)

    @pl.when(flags[0] > 0)
    def _():
        out_ref[0] = jnp.dot(scaled[...], own_ref[...], preferred_element_type=jnp.float32).astype(jnp.bfloat16)

    @pl.when(flags[0] == 0)
    def _():
        out_ref[0] = jnp.dot(scaled[...], src_ref[...], preferred_element_type=jnp.float32).astype(jnp.bfloat16)


def product(flags, x, gain, own, layer, src, blocks):
    tokens, depth = x.shape
    wide = 2 * HD
    return pl.pallas_call(
        product_kernel,
        out_shape=jax.ShapeDtypeStruct((blocks, tokens, wide), jnp.bfloat16),
        grid_spec=pltpu.PrefetchScalarGridSpec(
            num_scalar_prefetch=1,
            grid=(blocks,),
            in_specs=[
                pl.BlockSpec((tokens, depth), lambda j, f: (0, 0)),
                pl.BlockSpec((1, depth), lambda j, f: (0, 0)),
                pl.BlockSpec((None, None, depth, wide), lambda j, f: (0, layer, 0, f[1 + j] * f[0])),
                pl.BlockSpec((depth, wide), lambda j, f: (0, f[1 + j] * (1 - f[0]))),
            ],
            out_specs=pl.BlockSpec((1, tokens, wide), lambda j, f: (j, 0, 0)),
            scratch_shapes=[pltpu.VMEM((tokens, depth), jnp.bfloat16)],
        ),
        compiler_params=pltpu.CompilerParams(vmem_limit_bytes=32 * MIB),
        cost_estimate=pl.CostEstimate(
            flops=2 * tokens * depth * wide * blocks,
            bytes_accessed=2 * (tokens * depth + blocks * wide * (depth + tokens)),
            transcendentals=0,
        ),
    )(flags, x, gain, own, src)


def add(*terms):
    return sum(t.astype(jnp.float32) for t in terms)


def reduce_x(first, second):
    low = jnp.bfloat16
    plus = lax.ppermute(first[0:2], "tp", X_NEXT)
    minus = lax.ppermute(first[2:4], "tp", X_LAST)
    plus2 = lax.ppermute(add(second[0], plus[0]).astype(low), "tp", X_NEXT)
    minus2 = lax.ppermute(add(second[1], minus[0]).astype(low), "tp", X_LAST)
    away = add(second[2], minus[1], plus2).astype(low)
    mine = add(second[3], plus[1], minus2)
    return mine, lax.ppermute(away, "tp", H_SWAP)


def block_order():
    me = lax.axis_index("tp")
    h, x = me // NX, me % NX
    mine, other = h * NX, (1 - h) * NX
    nxt, last, far = (x + 1) % NX, (x + 3) % NX, (x + 2) % NX
    first = [other + far, mine + nxt, mine + far, other + last]
    second = [other + nxt, mine + last, other + x, mine + x]
    return first, second


def shards(hidden_first, hidden_second, weight_buffer, gain_buffer, loaded_layers, positions):
    inputs = (hidden_first, hidden_second)
    width = hidden_first.shape[1] * lax.axis_size("tp")
    tokens = hidden_first.shape[0]
    squares = jnp.stack([jnp.sum(jnp.square(v.astype(jnp.float32)), axis=1) for v in inputs])
    for pairs in (tp_pairs(lambda h, x: (h, x ^ 1)), tp_pairs(lambda h, x: (h, x ^ 2)), H_SWAP):
        squares = squares + lax.ppermute(squares, "tp", pairs)
    scale = lax.rsqrt(squares / width + 1e-05)
    half = HD // 2
    freq = 500000.0 ** (-2.0 * jnp.arange(half, dtype=jnp.float32) / HD)
    angle = positions.astype(jnp.float32)[:, None] * freq[None, :]
    cosine, sine = jnp.cos(angle), jnp.sin(angle)
    orders = block_order()
    results = []
    for layer in range(LAYERS):
        src = spread(weight_buffer[0, layer], gain_buffer[0, layer])
        own = (loaded_layers[0] > layer).astype(jnp.int32)
        parts = [
            product(jnp.stack([own] + order).astype(jnp.int32), inputs[layer], gain_buffer[0, layer][None, :], weight_buffer, layer, src, len(order))
            for order in orders
        ]
        mine, came = reduce_x(*parts)
        mixed = add(mine, came) * scale[layer][:, None]
        a, e, v = mixed[:, :half], mixed[:, half:HD], mixed[:, HD:]
        results.append(jnp.concatenate([a * cosine - e * sine, e * cosine + a * sine, v], axis=1).astype(jnp.bfloat16))
    return jnp.stack(results, axis=0)


def solution(mesh):
    placed = (
        P("chain", "tp"),
        P("chain", "tp"),
        P("chain", None, "tp", None),
        P("chain", None, "tp"),
        P("chain"),
        P("chain"),
    )
    return jax.shard_map(
        shards, mesh=mesh, in_specs=placed, out_specs=P(None, "chain", "tp"), check_vma=False
    )
```

```python
import jax
import jax.numpy as jnp
from jax import lax
from jax.experimental import pallas as pl
from jax.experimental.pallas import tpu as pltpu
from jax.sharding import PartitionSpec as P

HD = 128
WIDE = 2 * HD
LAYERS = 2
NY, NX, NZ = 4, 4, 4
VMEM = 56 << 20
TILES = 4
LOW = jnp.bfloat16


def flat(z, y, c, h, x):
    return ((z * NY + y % NY) * 2 + c) * 2 * NX + h * NX + x % NX


def tp_pairs(step):
    pairs = []
    for h in range(2):
        for x in range(NX):
            h2, x2 = step(h, x)
            pairs.append((h * NX + x, (h2 % 2) * NX + x2 % NX))
    return pairs


def chain_pairs(step):
    pairs = []
    for z in range(NZ):
        for y in range(NY):
            for c in range(2):
                to = step(z, y, c)
                if to is not None:
                    z2, y2, c2 = to
                    pairs.append(((z * NY + y) * 2 + c, (z2 * NY + y2 % NY) * 2 + c2))
    return pairs


X_NEXT = tp_pairs(lambda h, x: (h, x + 1))
X_LAST = tp_pairs(lambda h, x: (h, x - 1))
H_SWAP = tp_pairs(lambda h, x: (h + 1, x))
Z_FAR = chain_pairs(lambda z, y, c: (2, y, 0) if (z, c) == (0, 0) else None)
Z_NEAR = chain_pairs(lambda z, y, c: (z + 1, y, 0) if z in (0, 2) and c == 0 else None)
CORE = chain_pairs(lambda z, y, c: (z, y, 1) if c == 0 else None)
ROWS = [[z * NY * 2 + k for k in range(NY * 2)] for z in range(NZ)]


def diagonal(d):
    return [(flat(0, 0, 0, h, x), flat(0, d, 0, h, x - d)) for h in range(2) for x in range(NX)]


def after(value, *earlier):
    return lax.optimization_barrier((value, earlier))[0]


def place():
    tp, chain = lax.axis_index("tp"), lax.axis_index("chain")
    return tp // NX, tp % NX, chain // (2 * NY), chain // 2 % NY, chain % 2


def pieces(weights, gains, layers, head_row):
    x = lax.axis_index("tp") % NX
    out = []
    for d in range(NX):
        column = (head_row * NX + (x - d) % NX) * WIDE
        parts = []
        for layer in layers:
            block = lax.dynamic_slice_in_dim(weights[0, layer], column, WIDE, 1).astype(jnp.float32)
            parts.append((block * gains[0, layer][:, None].astype(jnp.float32)).astype(LOW))
        out.append(jnp.stack(parts))
    return out


def scatter(parts):
    _, _, _, y, _ = place()
    got = {d: lax.ppermute(parts[d], ("chain", "tp"), diagonal(d)) for d in (2, 1, 3)}
    return jnp.where(y == 0, parts[0], jnp.where(y == 1, got[1], jnp.where(y == 2, got[2], got[3])))


def down(first):
    _, _, z, _, c = place()
    far = lax.ppermute(first, "chain", Z_FAR)
    second = jnp.where(z == 2, far, first)
    near = lax.ppermute(second, "chain", Z_NEAR)
    mine = jnp.where((z == 1) | (z == 3), near, second)
    cut = mine.shape[1] // 2
    other = lax.ppermute(mine[:, cut:], "chain", CORE)
    return jnp.where(c == 0, mine[:, :cut], other)


def gather(half):
    return lax.all_gather(half, "chain", axis_index_groups=ROWS, axis=0)


def scaled_of(x, gain):
    return (x.astype(jnp.float32) * gain.astype(jnp.float32)).astype(LOW)


def dot(a, b):
    return jnp.dot(a, b, preferred_element_type=jnp.float32)


def build_kernel(flags, x_ref, g_ref, own_ref, plus_ref, minus_ref, scaled):
    j = pl.program_id(0)
    held = flags[0] > 0

    @pl.when(held & (j == 0))
    def _():
        scaled[...] = scaled_of(x_ref[...], g_ref[...])

    def put(out_ref):
        @pl.when(held)
        def _():
            out_ref[0] = dot(scaled[...], own_ref[...]).astype(LOW)

        for slot in range(NX):
            @pl.when(jnp.logical_not(held) & (j % NX == slot))
            def _():
                out_ref[0] = x_ref[:, slot * WIDE:(slot + 1) * WIDE]

    @pl.when(j < NX)
    def _():
        put(plus_ref)

    @pl.when(j >= NX)
    def _():
        put(minus_ref)


def build(held, x, gain, own, layer):
    tokens, depth = x.shape
    h, here, _, _, _ = place()
    mine, other = h * NX, (1 - h) * NX
    nxt, last, far = (here + 1) % NX, (here + 3) % NX, (here + 2) % NX
    order = [other + nxt, mine + nxt, other + far, other + far, mine + far, mine + far, other + last, mine + last]
    flags = jnp.stack([held] + order).astype(jnp.int32)
    shape = jax.ShapeDtypeStruct((NX, tokens, WIDE), LOW)
    return pl.pallas_call(
        build_kernel,
        out_shape=(shape, shape),
        grid_spec=pltpu.PrefetchScalarGridSpec(
            num_scalar_prefetch=1,
            grid=(2 * NX,),
            in_specs=[
                pl.BlockSpec((tokens, depth), lambda j, f: (0, 0)),
                pl.BlockSpec((1, depth), lambda j, f: (0, 0)),
                pl.BlockSpec((None, None, depth, WIDE), lambda j, f: (0, layer, 0, f[1 + j] * f[0])),
            ],
            out_specs=(
                pl.BlockSpec((1, tokens, WIDE), lambda j, f: (jnp.minimum(j, NX - 1), 0, 0)),
                pl.BlockSpec((1, tokens, WIDE), lambda j, f: (jnp.maximum(j - NX, 0), 0, 0)),
            ),
            scratch_shapes=[pltpu.VMEM((tokens, depth), LOW)],
        ),
        compiler_params=pltpu.CompilerParams(vmem_limit_bytes=VMEM),
        cost_estimate=pl.CostEstimate(
            flops=2 * tokens * depth * WIDE * 2 * NX, bytes_accessed=12 * tokens * depth, transcendentals=0
        ),
    )(flags, x, gain, own)


def head_sum(mine, flags, refs, scaled):
    x_ref, g_ref, own_ref, plus_ref, minus_ref, pass_plus, pass_minus, src_ref, acc = refs

    @pl.when(flags[0] > 0)
    def _():
        total = dot(scaled_of(x_ref[...], g_ref[...]), own_ref[...])
        late = pass_minus if mine else pass_plus
        for term in (plus_ref[1 if mine else 0], minus_ref[3 if mine else 2], late[0]):
            total += term.astype(jnp.float32)
        acc[...] = total

    @pl.when(flags[0] == 0)
    def _():
        total = dot(x_ref[:, :2 * WIDE], src_ref[0]) + dot(x_ref[:, 2 * WIDE:], src_ref[1])
        blocks = [minus_ref[s] for s in range(NX)]
        blocks += [pass_minus[0], pass_minus[1], pass_plus[0], pass_plus[1]]
        blocks += [plus_ref[s] for s in range(NX)]
        for k, block in enumerate(blocks):
            total += dot(block, src_ref[2 + k // 2, (k % 2) * WIDE:(k % 2 + 1) * WIDE, :])
        acc[...] = total


def away_kernel(flags, *refs):
    *head, out_ref, acc = refs
    head_sum(False, flags, (*head, acc), None)
    out_ref[...] = acc[...].astype(LOW)


def mine_kernel(flags, *refs):
    *head, came_ref, scale_ref, cos_ref, sin_ref, _, out_ref, acc = refs
    head_sum(True, flags, (*head, acc), None)
    mixed = (acc[...] + came_ref[...].astype(jnp.float32)) * scale_ref[...]
    key = mixed[:, :HD]
    out_ref[:, :HD] = (key * cos_ref[...] + pltpu.roll(key, HD // 2, 1) * sin_ref[...]).astype(LOW)
    out_ref[:, HD:] = mixed[:, HD:].astype(LOW)


def finish(held, x, gain, own, layer, moved, src, src_layer, rest=None):
    tokens, depth = x.shape
    tile = tokens // TILES
    h, here, _, _, _ = place()
    head = (h if rest is not None else 1 - h) * NX + here
    flags = jnp.stack([held, head]).astype(jnp.int32)
    slots = pl.BlockSpec((NX, tile, WIDE), lambda i, f: (0, i, 0))
    passed = pl.BlockSpec((2, tile, WIDE), lambda i, f: (0, i, 0))
    in_specs = [
        pl.BlockSpec((tile, depth), lambda i, f: (i, 0)),
        pl.BlockSpec((1, depth), lambda i, f: (0, 0)),
        pl.BlockSpec((None, None, depth, WIDE), lambda i, f: (0, layer, 0, f[1])),
        slots,
        slots,
        passed,
        passed,
        pl.BlockSpec((2 * NY, None, depth // 2, WIDE), lambda i, f: (0, src_layer, 0, 0)),
    ]
    args = [x, gain, own, *moved, src]
    aliases = {}
    if rest is None:
        kernel = away_kernel
        out_shape = jax.ShapeDtypeStruct((tokens, WIDE), LOW)
        out_specs = pl.BlockSpec((tile, WIDE), lambda i, f: (i, 0))
    else:
        kernel = mine_kernel
        came, scale, cosine, sine, out = rest
        wide = pl.BlockSpec((tile, HD), lambda i, f: (i, 0))
        in_specs += [
            pl.BlockSpec((tile, WIDE), lambda i, f: (i, 0)),
            pl.BlockSpec((tile, 1), lambda i, f: (i, 0)),
            wide,
            wide,
            pl.BlockSpec(memory_space=pl.ANY),
        ]
        args += [came, scale, cosine, sine, out]
        out_shape = jax.ShapeDtypeStruct((LAYERS, tokens, WIDE), LOW)
        out_specs = pl.BlockSpec((None, tile, WIDE), lambda i, f: (layer, i, 0))
        if layer > 0:
            aliases = {len(args): 0}
    return pl.pallas_call(
        kernel,
        out_shape=out_shape,
        grid_spec=pltpu.PrefetchScalarGridSpec(
            num_scalar_prefetch=1,
            grid=(TILES,),
            in_specs=in_specs,
            out_specs=out_specs,
            scratch_shapes=[pltpu.VMEM((tile, WIDE), jnp.float32)],
        ),
        input_output_aliases=aliases,
        compiler_params=pltpu.CompilerParams(vmem_limit_bytes=VMEM),
        cost_estimate=pl.CostEstimate(
            flops=2 * tokens * 4 * depth * WIDE, bytes_accessed=10 * tokens * depth, transcendentals=0
        ),
    )(flags, *args)


def ring_start(sent):
    plus, minus = sent
    return lax.ppermute(plus, "tp", X_NEXT), lax.ppermute(minus, "tp", X_LAST)


def ring_pass(got):
    plus, minus = got
    return lax.ppermute(plus[2:], "tp", X_NEXT), lax.ppermute(minus[:2], "tp", X_LAST)


def shards(hidden_first, hidden_second, weight_buffer, gain_buffer, loaded_layers, positions):
    inputs = (hidden_first, hidden_second)
    width = hidden_first.shape[1] * lax.axis_size("tp")
    h = lax.axis_index("tp") // NX
    held = [(loaded_layers[0] > layer).astype(jnp.int32) for layer in range(LAYERS)]
    gains = [gain_buffer[0, layer][None, :] for layer in range(LAYERS)]

    swap0 = scatter(pieces(weight_buffer, gain_buffer, (0,), 1 - h))
    sent0 = build(held[0], inputs[0], gains[0], weight_buffer, 0)
    got0 = ring_start(sent0)
    sent1 = build(held[1], inputs[1], gains[1], weight_buffer, 1)

    squares = jnp.stack([jnp.sum(jnp.square(v.astype(jnp.float32)), axis=1) for v in inputs])
    for pairs in (tp_pairs(lambda h, x: (h, x ^ 1)), tp_pairs(lambda h, x: (h, x ^ 2)), H_SWAP):
        squares = squares + lax.ppermute(squares, "tp", pairs)
    scale = lax.rsqrt(squares / width + 1e-05)
    half = HD // 2
    freq = 500000.0 ** (-2.0 * jnp.arange(half, dtype=jnp.float32) / HD)
    angle = positions.astype(jnp.float32)[:, None] * freq[None, :]
    cosine, sine = jnp.cos(angle), jnp.sin(angle)
    cosine, sine = jnp.concatenate([cosine, cosine], 1), jnp.concatenate([-sine, sine], 1)

    weights1, gains1 = after((weight_buffer, gain_buffer), swap0)
    swap1 = scatter(pieces(weights1, gains1, (1,), 1 - h))
    half0 = down(swap0)
    src0 = gather(half0)
    weights2, gains2 = after((weight_buffer, gain_buffer), swap1)
    keep = scatter(pieces(weights2, gains2, (0, 1), h))
    half1 = down(swap1)
    src1 = gather(half1)
    passed0 = ring_pass(after(got0, half0))
    got1 = ring_start(after(sent1, passed0))
    half2 = down(keep)
    src2 = gather(half2)
    passed1 = ring_pass(after(got1, half2))

    away0 = finish(held[0], inputs[0], gains[0], weight_buffer, 0, (*got0, *passed0), src0, 0)
    came0 = lax.ppermute(away0, "tp", H_SWAP)
    away1 = finish(held[1], inputs[1], gains[1], weight_buffer, 1, (*got1, *passed1), src1, 0)
    came1 = lax.ppermute(away1, "tp", H_SWAP)
    out = jnp.zeros((8, 128), LOW)
    for layer, (got, passed, came) in enumerate(((got0, passed0, came0), (got1, passed1, came1))):
        rest = (came, scale[layer][:, None], cosine, sine, out)
        out = finish(held[layer], inputs[layer], gains[layer], weight_buffer, layer, (*got, *passed), src2, layer, rest)
    return out


def solution(mesh):
    placed = (
        P("chain", "tp"),
        P("chain", "tp"),
        P("chain", None, "tp", None),
        P("chain", None, "tp"),
        P("chain"),
        P("chain"),
    )
    return jax.shard_map(
        shards, mesh=mesh, in_specs=placed, out_specs=P(None, "chain", "tp"), check_vma=False
    )
```

```python
import functools

import jax
import jax.numpy as jnp
from jax import lax
from jax.experimental import pallas as pl
from jax.experimental.pallas import tpu as pltpu
from jax.sharding import PartitionSpec as P

HD = 128
WIDE = 2 * HD
LAYERS = 2
NY, NX, NZ = 4, 4, 4
VMEM = 56 << 20
LOW = jnp.bfloat16
COLUMNS = LAYERS


def tp_pairs(step):
    pairs = []
    for h in range(2):
        for x in range(NX):
            h2, x2 = step(h, x)
            pairs.append((h * NX + x, (h2 % 2) * NX + x2 % NX))
    return pairs


def chain_pairs(step):
    pairs = []
    for z in range(NZ):
        for y in range(NY):
            for c in range(2):
                to = step(z, y, c)
                if to is not None:
                    z2, y2, c2 = to
                    pairs.append(((z * NY + y) * 2 + c, (z2 * NY + y2 % NY) * 2 + c2))
    return pairs


X_NEXT = tp_pairs(lambda h, x: (h, x + 1))
X_LAST = tp_pairs(lambda h, x: (h, x - 1))
X_ONE = tp_pairs(lambda h, x: (h, x ^ 1))
X_TWO = tp_pairs(lambda h, x: (h, x ^ 2))
H_SWAP = tp_pairs(lambda h, x: (h + 1, x))
Z_FAR = chain_pairs(lambda z, y, c: (2, y, 0) if (z, c) == (0, 0) else None)
Z_NEAR = chain_pairs(lambda z, y, c: (z + 1, y, 0) if z in (0, 2) and c == 0 else None)
CORE = chain_pairs(lambda z, y, c: (z, y, 1) if c == 0 else None)
ROWS = [[z * NY * 2 + k for k in range(NY * 2)] for z in range(NZ)]


def from_source(k):
    return chain_pairs(lambda z, y, c: (0, k, 0) if (z, y, c) == (0, 0, 0) else None)


def after(value, *earlier):
    return lax.optimization_barrier((value, earlier))[0]


def place():
    tp, chain = lax.axis_index("tp"), lax.axis_index("chain")
    return tp // NX, tp % NX, chain // (2 * NY), chain // 2 % NY, chain % 2


def dot(a, b):
    return jnp.dot(a, b, preferred_element_type=jnp.float32)


def pieces_kernel(flags, w_ref, g_ref, *out_refs):
    for layer in range(LAYERS):
        row = g_ref[layer:layer + 1, :].astype(jnp.float32)
        gain = jnp.broadcast_to(row, (HD, row.shape[1])).T
        depth = row.shape[1] // NY
        for y, out_ref in enumerate(out_refs):
            rows = slice(y * depth, (y + 1) * depth)
            for at in range(0, w_ref.shape[2], HD):
                out_ref[layer, :, at:at + HD] = (w_ref[layer, rows, at:at + HD].astype(jnp.float32) * gain[rows]).astype(LOW)


def pieces(flags, weights, gains, which):
    depth, wide = weights.shape[2], weights.shape[3] // 2
    return pl.pallas_call(
        pieces_kernel,
        out_shape=tuple(jax.ShapeDtypeStruct((LAYERS, depth // NY, wide), LOW) for _ in range(NY)),
        grid_spec=pltpu.PrefetchScalarGridSpec(
            num_scalar_prefetch=1,
            grid=(1,),
            in_specs=[
                pl.BlockSpec((None, LAYERS, depth, wide), lambda i, f: (0, 0, 0, f[COLUMNS + which * NX] // NX)),
                pl.BlockSpec((None, LAYERS, depth), lambda i, f: (0, 0, 0)),
            ],
            out_specs=tuple(pl.BlockSpec((LAYERS, depth // NY, wide), lambda i, f: (0, 0, 0)) for _ in range(NY)),
        ),
        compiler_params=pltpu.CompilerParams(vmem_limit_bytes=VMEM),
        cost_estimate=pl.CostEstimate(
            flops=LAYERS * depth * wide, bytes_accessed=4 * LAYERS * depth * wide, transcendentals=0
        ),
    )(flags, weights, gains)


def scatter(parts):
    y = place()[3]
    got = {k: lax.ppermute(parts[k], "chain", from_source(k)) for k in (2, 1, 3)}
    return jnp.where(y == 0, parts[0], jnp.where(y == 1, got[1], jnp.where(y == 2, got[2], got[3])))


def down(first):
    z = place()[2]
    far = lax.ppermute(first, "chain", Z_FAR)
    second = jnp.where(z == 2, far, first)
    near = lax.ppermute(second, "chain", Z_NEAR)
    return jnp.where((z == 1) | (z == 3), near, second)


def across(mine):
    cut = mine.shape[1] // 2
    other = lax.ppermute(mine[:, cut:], "chain", CORE)
    return jnp.where(place()[4] == 0, mine[:, :cut], other)


def gather(half):
    return lax.all_gather(half, "chain", axis_index_groups=ROWS, axis=0)


def product_kernel(layer, flags, x_ref, g_ref, own_ref, src_ref, plus_ref, minus_ref, keep_ref, scaled):
    j = pl.program_id(0)
    held = flags[layer] > 0
    cut = x_ref.shape[0] // 2

    @pl.when(j == 0)
    def _():
        gain = jnp.where(held, g_ref[layer:layer + 1, :].astype(jnp.float32), 1.0)
        scaled[...] = (x_ref[...].astype(jnp.float32) * gain).astype(LOW)

    def put(weights):
        total = dot(scaled[...], weights).astype(LOW)
        low, high = total[:cut], total[cut:]

        @pl.when(j == 0)
        def _():
            plus_ref[0] = low
            minus_ref[0] = high

        @pl.when(j == 1)
        def _():
            plus_ref[1] = high
            keep_ref[0] = low

        @pl.when(j == 2)
        def _():
            minus_ref[1] = low
            keep_ref[1] = high

        @pl.when(j == 3)
        def _():
            keep_ref[2] = low
            keep_ref[3] = high

    @pl.when(held)
    def _():
        put(own_ref[...])

    @pl.when(jnp.logical_not(held))
    def _():
        put(src_ref[...].reshape(own_ref.shape))


def product(flags, x, gain, own, layer, src, which):
    tokens, depth = x.shape
    first = COLUMNS + which * NX

    def whole(*shape):
        return pl.BlockSpec(shape, lambda j, f: (0,) * len(shape))

    shapes = [(2, tokens // 2, WIDE), (2, tokens // 2, WIDE), (4, tokens // 2, WIDE)]
    return pl.pallas_call(
        functools.partial(product_kernel, layer),
        out_shape=tuple(jax.ShapeDtypeStruct(shape, LOW) for shape in shapes),
        grid_spec=pltpu.PrefetchScalarGridSpec(
            num_scalar_prefetch=1,
            grid=(NX,),
            in_specs=[
                whole(tokens, depth),
                pl.BlockSpec((None, LAYERS, depth), lambda j, f: (0, 0, 0)),
                pl.BlockSpec((None, None, depth, WIDE), lambda j, f: (0, layer, 0, f[first + j * f[layer]])),
                pl.BlockSpec((2 * NY, None, depth // (2 * NY), WIDE), lambda j, f: (0, layer, 0, f[first + j * (1 - f[layer])] % NX)),
            ],
            out_specs=tuple(whole(*shape) for shape in shapes),
            scratch_shapes=[pltpu.VMEM((tokens, depth), LOW)],
        ),
        compiler_params=pltpu.CompilerParams(vmem_limit_bytes=VMEM),
        cost_estimate=pl.CostEstimate(
            flops=2 * tokens * depth * WIDE * NX,
            bytes_accessed=2 * (tokens * depth + NX * WIDE * (depth + tokens)),
            transcendentals=0,
        ),
    )(flags, x, gain, own, src)


def add(*terms):
    return sum(t.astype(jnp.float32) for t in terms)


def round_x(plus, minus, keep):
    plus1 = lax.ppermute(plus, "tp", X_NEXT)
    minus1 = lax.ppermute(minus, "tp", X_LAST)
    plus2 = lax.ppermute(add(keep[0], plus1[0]).astype(LOW), "tp", X_NEXT)
    minus2 = lax.ppermute(add(keep[1], minus1[0]).astype(LOW), "tp", X_LAST)
    return keep, plus1, minus1, plus2, minus2


def swapped(keep, plus1, minus1, plus2, minus2):
    low = add(keep[2], plus2, minus1[1])
    high = add(keep[3], minus2, plus1[1])
    return lax.ppermute(jnp.stack([low, high]).astype(LOW), "tp", H_SWAP)


def close_kernel(keep_ref, plus1, minus1, plus2, minus2, came_ref, cos_ref, sin_ref, scale_ref, *refs):
    out_ref = refs[-1]
    cut = keep_ref.shape[1]
    for i, (one, two) in enumerate(((minus1, plus2), (plus1, minus2))):
        rows = slice(i * cut, (i + 1) * cut)
        total = add(keep_ref[2 + i], one[1], two[...], came_ref[i])
        key = total[:, :HD]
        turned = key * cos_ref[rows, :] + pltpu.roll(key, HD // 2, 1) * sin_ref[rows, :]
        out_ref[rows, :HD] = turned.astype(LOW)
        out_ref[rows, HD:] = (total[:, HD:] * scale_ref[rows, :]).astype(LOW)


def close(layer, terms, came, turns, out):
    tokens = turns[0].shape[0]
    args = [*terms, came, *turns]
    in_specs = [pl.BlockSpec(a.shape, lambda i, n=a.ndim: (0,) * n) for a in args]
    aliases = {}
    if out is not None:
        aliases = {len(args): 0}
        args.append(out)
        in_specs.append(pl.BlockSpec(memory_space=pl.ANY))
    return pl.pallas_call(
        close_kernel,
        out_shape=jax.ShapeDtypeStruct((LAYERS, tokens, WIDE), LOW),
        grid=(1,),
        in_specs=in_specs,
        out_specs=pl.BlockSpec((None, tokens, WIDE), lambda i: (layer, 0, 0)),
        input_output_aliases=aliases,
        compiler_params=pltpu.CompilerParams(vmem_limit_bytes=VMEM),
        cost_estimate=pl.CostEstimate(flops=8 * tokens * WIDE, bytes_accessed=16 * tokens * WIDE, transcendentals=0),
    )(*args)


def flags_of(loaded_layers):
    h, x = place()[:2]
    flags = [(loaded_layers[0] > layer).astype(jnp.int32) for layer in range(LAYERS)]
    flags += [row * NX + (x + d) % NX for row in (1 - h, h) for d in (2, 1, 3, 0)]
    return jnp.stack(flags).astype(jnp.int32)


def turns_of(squares, width, positions):
    scale = lax.rsqrt(squares / width + 1e-05)[:, :, None]
    half = HD // 2
    freq = 500000.0 ** (-2.0 * jnp.arange(half, dtype=jnp.float32) / HD)
    angle = positions.astype(jnp.float32)[:, None] * freq[None, :]
    cosine, sine = jnp.cos(angle), jnp.sin(angle)
    cosine, sine = jnp.concatenate([cosine, cosine], 1), jnp.concatenate([-sine, sine], 1)
    return [(cosine * s, sine * s, jnp.broadcast_to(s, cosine.shape)) for s in scale]


def shards(hidden_first, hidden_second, weight_buffer, gain_buffer, loaded_layers, positions):
    inputs = (hidden_first, hidden_second)
    width = hidden_first.shape[1] * lax.axis_size("tp")
    flags = flags_of(loaded_layers)
    swap_parts = pieces(flags, weight_buffer, gain_buffer, 0)
    swap = scatter(swap_parts)
    keep_parts = pieces(flags, weight_buffer, gain_buffer, 1)
    squares = jnp.stack([jnp.sum(jnp.square(v.astype(jnp.float32)), axis=1) for v in inputs])

    swap, keep_parts, squares = lax.optimization_barrier((swap, keep_parts, squares))
    keep = scatter(keep_parts)
    swap = down(swap)
    swap, keep, squares = lax.optimization_barrier((swap, keep, squares))
    swap_half = across(swap)
    swap_src = gather(swap_half)
    keep = down(after(keep, swap_half))
    for pairs in (X_ONE, X_TWO, H_SWAP):
        squares = squares + lax.ppermute(squares, "tp", pairs)
    turns = turns_of(squares, width, positions)
    keep, turns = lax.optimization_barrier((keep, turns))
    keep_src = gather(across(keep))

    def sums(layer, src, which):
        return product(flags, inputs[layer], gain_buffer, weight_buffer, layer, src, which)

    came = [swapped(*round_x(*sums(layer, swap_src, 0))) for layer in range(LAYERS)]
    out = None
    for layer in range(LAYERS):
        out = close(layer, round_x(*sums(layer, keep_src, 1)), came[layer], turns[layer], out)
    return out


def solution(mesh):
    placed = (
        P("chain", "tp"),
        P("chain", "tp"),
        P("chain", None, "tp", None),
        P("chain", None, "tp"),
        P("chain"),
        P("chain"),
    )
    return jax.shard_map(
        shards, mesh=mesh, in_specs=placed, out_specs=P(None, "chain", "tp"), check_vma=False
    )
```

```python
import functools

import jax
import jax.numpy as jnp
from jax import lax
from jax.experimental import pallas as pl
from jax.experimental.pallas import tpu as pltpu
from jax.sharding import PartitionSpec as P

HD = 128
WIDE = 2 * HD
LAYERS = 2
NY, NX, NZ = 4, 4, 4
VMEM_LARGE, VMEM_SMALL = 52 << 20, 20 << 20
LOW = jnp.bfloat16
COLUMNS = LAYERS


def tp_pairs(step):
    pairs = []
    for h in range(2):
        for x in range(NX):
            h2, x2 = step(h, x)
            pairs.append((h * NX + x, (h2 % 2) * NX + x2 % NX))
    return pairs


def chain_pairs(step):
    pairs = []
    for z in range(NZ):
        for y in range(NY):
            for c in range(2):
                to = step(z, y, c)
                if to is not None:
                    z2, y2, c2 = to
                    pairs.append(((z * NY + y) * 2 + c, (z2 * NY + y2 % NY) * 2 + c2))
    return pairs


X_NEXT = tp_pairs(lambda h, x: (h, x + 1))
X_LAST = tp_pairs(lambda h, x: (h, x - 1))
X_ONE = tp_pairs(lambda h, x: (h, x ^ 1))
X_TWO = tp_pairs(lambda h, x: (h, x ^ 2))
H_SWAP = tp_pairs(lambda h, x: (h + 1, x))
Z_FAR = chain_pairs(lambda z, y, c: (2, y, 0) if (z, c) == (0, 0) else None)
Z_NEAR = chain_pairs(lambda z, y, c: (z + 1, y, 0) if z in (0, 2) and c == 0 else None)
CORE = chain_pairs(lambda z, y, c: (z, y, 1) if c == 0 else None)
ROWS = [[z * NY * 2 + k for k in range(NY * 2)] for z in range(NZ)]


def from_source(k):
    return chain_pairs(lambda z, y, c: (0, k, 0) if (z, y, c) == (0, 0, 0) else None)


def after(value, *earlier):
    return lax.optimization_barrier((value, earlier))[0]


def place():
    tp, chain = lax.axis_index("tp"), lax.axis_index("chain")
    return tp // NX, tp % NX, chain // (2 * NY), chain // 2 % NY, chain % 2


def dot(a, b):
    return jnp.dot(a, b, preferred_element_type=jnp.float32)


def pieces_kernel(flags, w_ref, g_ref, *refs):
    out_refs, raw, sems = refs[:NY], refs[NY], refs[NY + 1]
    depth, wide = out_refs[0].shape[1:]
    column = pl.multiple_of(flags[0] * wide, wide)

    def read(y):
        rows = pl.ds(y * depth, depth)
        return pltpu.make_async_copy(w_ref.at[0, :, rows, pl.ds(column, wide)], raw.at[y], sems.at[y])

    order = (2, 1, 3, 0)
    for y in order:
        read(y).start()
    gains = []
    for layer in range(LAYERS):
        row = g_ref[0, layer:layer + 1, :].astype(jnp.float32)
        gains.append(jnp.broadcast_to(row, (HD, row.shape[1])).T)
    for y in order:
        read(y).wait()
        for layer in range(LAYERS):
            gain = gains[layer][y * depth:(y + 1) * depth]
            for at in range(0, wide, HD):
                out_refs[y][layer, :, at:at + HD] = (raw[y, layer, :, at:at + HD].astype(jnp.float32) * gain).astype(LOW)


def pieces(weights, gains, row):
    depth, wide = weights.shape[2] // NY, weights.shape[3] // 2
    vmem = pl.BlockSpec(memory_space=pltpu.VMEM)
    shape = (LAYERS, depth, wide)
    return pl.pallas_call(
        pieces_kernel,
        out_shape=tuple(jax.ShapeDtypeStruct(shape, LOW) for _ in range(NY)),
        in_specs=[pl.BlockSpec(memory_space=pltpu.SMEM), pl.BlockSpec(memory_space=pltpu.HBM), vmem],
        out_specs=tuple(vmem for _ in range(NY)),
        scratch_shapes=[pltpu.VMEM((NY, *shape), LOW), pltpu.SemaphoreType.DMA((NY,))],
        compiler_params=pltpu.CompilerParams(vmem_limit_bytes=VMEM_LARGE),
        cost_estimate=pl.CostEstimate(
            flops=LAYERS * NY * depth * wide, bytes_accessed=4 * LAYERS * NY * depth * wide, transcendentals=0
        ),
    )(row.astype(jnp.int32).reshape(1), weights, gains)


def scatter(parts):
    y = place()[3]
    got = {k: lax.ppermute(parts[k], "chain", from_source(k)) for k in (2, 1, 3)}
    return jnp.where(y == 0, parts[0], jnp.where(y == 1, got[1], jnp.where(y == 2, got[2], got[3])))


def down(first):
    z = place()[2]
    far = lax.ppermute(first, "chain", Z_FAR)
    second = jnp.where(z == 2, far, first)
    near = lax.ppermute(second, "chain", Z_NEAR)
    return jnp.where((z == 1) | (z == 3), near, second)


def across(mine):
    cut = mine.shape[1] // 2
    other = lax.ppermute(mine[:, cut:], "chain", CORE)
    return jnp.where(place()[4] == 0, mine[:, :cut], other)


def gather(half):
    return lax.all_gather(half, "chain", axis_index_groups=ROWS, axis=0)


def product_kernel(layer, first, flags, x_ref, own_ref, src_ref, plus_ref, minus_ref, keep_ref, blocks, sems):
    held = flags[layer] > 0
    cut = x_ref.shape[0] // 2
    for j in range(NX):
        head = flags[first + j]

        @pl.when(held)
        def _():
            column = pl.ds(pl.multiple_of(head * WIDE, WIDE), WIDE)
            pltpu.make_async_copy(own_ref.at[0, layer, :, :, column], blocks.at[j], sems.at[j]).start()

        @pl.when(jnp.logical_not(held))
        def _():
            column = pl.ds(pl.multiple_of(head % NX * WIDE, WIDE), WIDE)
            pltpu.make_async_copy(src_ref.at[:, layer, :, column], blocks.at[j], sems.at[j]).start()

    low, high = slice(0, cut), slice(cut, 2 * cut)
    goals = (
        ((plus_ref, 0, low), (minus_ref, 0, high)),
        ((plus_ref, 1, high), (keep_ref, 0, low)),
        ((minus_ref, 1, low), (keep_ref, 1, high)),
        ((keep_ref, 2, low), (keep_ref, 3, high)),
    )
    for j, goal in enumerate(goals):
        pltpu.make_async_copy(src_ref.at[:, layer, :, pl.ds(0, WIDE)], blocks.at[j], sems.at[j]).wait()
        block = blocks[j].reshape(-1, WIDE)
        for ref, slot, rows in goal:
            ref[slot] = dot(x_ref[rows, :], block).astype(LOW)


def product(flags, x, own, layer, src, which):
    tokens, depth = x.shape
    shapes = [(2, tokens // 2, WIDE), (2, tokens // 2, WIDE), (4, tokens // 2, WIDE)]
    vmem, hbm = pl.BlockSpec(memory_space=pltpu.VMEM), pl.BlockSpec(memory_space=pltpu.HBM)
    return pl.pallas_call(
        functools.partial(product_kernel, layer, COLUMNS + which * NX),
        out_shape=tuple(jax.ShapeDtypeStruct(shape, LOW) for shape in shapes),
        in_specs=[pl.BlockSpec(memory_space=pltpu.SMEM), vmem, hbm, hbm],
        out_specs=(vmem, vmem, vmem),
        scratch_shapes=[
            pltpu.VMEM((NX, 2 * NY, depth // (2 * NY), WIDE), LOW),
            pltpu.SemaphoreType.DMA((NX,)),
        ],
        compiler_params=pltpu.CompilerParams(vmem_limit_bytes=VMEM_LARGE),
        cost_estimate=pl.CostEstimate(
            flops=2 * tokens * depth * WIDE * NX,
            bytes_accessed=2 * (tokens * depth + NX * WIDE * (depth + tokens)),
            transcendentals=0,
        ),
    )(flags, x, own, src)


def add(*terms):
    return sum(t.astype(jnp.float32) for t in terms)


def round_x(plus, minus, keep):
    plus1 = lax.ppermute(plus, "tp", X_NEXT)
    minus1 = lax.ppermute(minus, "tp", X_LAST)
    plus2 = lax.ppermute(add(keep[0], plus1[0]).astype(LOW), "tp", X_NEXT)
    minus2 = lax.ppermute(add(keep[1], minus1[0]).astype(LOW), "tp", X_LAST)
    return keep, plus1, minus1, plus2, minus2


def swapped(keep, plus1, minus1, plus2, minus2):
    low = add(keep[2], plus2, minus1[1])
    high = add(keep[3], minus2, plus1[1])
    return lax.ppermute(jnp.stack([low, high]).astype(LOW), "tp", H_SWAP)


def close_kernel(keep_ref, plus1, minus1, plus2, minus2, came_ref, cos_ref, sin_ref, scale_ref, *refs):
    out_ref = refs[-1]
    cut = keep_ref.shape[1]
    for i, (one, two) in enumerate(((minus1, plus2), (plus1, minus2))):
        rows = slice(i * cut, (i + 1) * cut)
        total = add(keep_ref[2 + i], one[1], two[...], came_ref[i])
        key = total[:, :HD]
        turned = key * cos_ref[rows, :] + pltpu.roll(key, HD // 2, 1) * sin_ref[rows, :]
        out_ref[rows, :HD] = turned.astype(LOW)
        out_ref[rows, HD:] = (total[:, HD:] * scale_ref[rows, :]).astype(LOW)


def close(layer, terms, came, turns, out):
    tokens = turns[0].shape[0]
    args = [*terms, came, *turns]
    in_specs = [pl.BlockSpec(memory_space=pltpu.VMEM) for _ in args]
    aliases = {}
    if out is not None:
        aliases = {len(args): 0}
        args.append(out)
        in_specs.append(pl.BlockSpec(memory_space=pl.ANY))
    return pl.pallas_call(
        close_kernel,
        out_shape=jax.ShapeDtypeStruct((LAYERS, tokens, WIDE), LOW),
        grid=(1,),
        in_specs=in_specs,
        out_specs=pl.BlockSpec((None, tokens, WIDE), lambda i: (layer, 0, 0)),
        input_output_aliases=aliases,
        compiler_params=pltpu.CompilerParams(vmem_limit_bytes=VMEM_SMALL),
        cost_estimate=pl.CostEstimate(flops=8 * tokens * WIDE, bytes_accessed=16 * tokens * WIDE, transcendentals=0),
    )(*args)


def flags_of(loaded_layers):
    h, x = place()[:2]
    flags = [(loaded_layers[0] > layer).astype(jnp.int32) for layer in range(LAYERS)]
    flags += [row * NX + (x + d) % NX for row in (1 - h, h) for d in (2, 1, 3, 0)]
    return jnp.stack(flags).astype(jnp.int32)


def turns_of(squares, width, positions):
    scale = lax.rsqrt(squares / width + 1e-05)[:, :, None]
    half = HD // 2
    freq = 500000.0 ** (-2.0 * jnp.arange(half, dtype=jnp.float32) / HD)
    angle = positions.astype(jnp.float32)[:, None] * freq[None, :]
    cosine, sine = jnp.cos(angle), jnp.sin(angle)
    cosine, sine = jnp.concatenate([cosine, cosine], 1), jnp.concatenate([-sine, sine], 1)
    return [(cosine * s, sine * s, jnp.broadcast_to(s, cosine.shape)) for s in scale]


def shards(hidden_first, hidden_second, weight_buffer, gain_buffer, loaded_layers, positions):
    inputs = (hidden_first, hidden_second)
    width = hidden_first.shape[1] * lax.axis_size("tp")
    flags = flags_of(loaded_layers)
    h = place()[0]
    own = weight_buffer.reshape(1, LAYERS, 2 * NY, -1, weight_buffer.shape[3])
    swap = scatter(pieces(weight_buffer, gain_buffer, 1 - h))
    keep_parts = pieces(weight_buffer, gain_buffer, h)
    wide = [v.astype(jnp.float32) for v in inputs]
    squares = jnp.stack([jnp.sum(jnp.square(v), axis=1) for v in wide])
    scaled = [
        jnp.where(loaded_layers[0] > layer, (v * gain_buffer[0, layer][None, :].astype(jnp.float32)).astype(LOW), inputs[layer])
        for layer, v in enumerate(wide)
    ]

    swap, keep_parts, squares, scaled = lax.optimization_barrier((swap, keep_parts, squares, scaled))
    keep = scatter(keep_parts)
    swap = down(swap)
    swap, keep = lax.optimization_barrier((swap, keep))
    swap_half = across(swap)
    swap_src = gather(swap_half)
    keep = down(after(keep, swap_half))
    squares = after(squares, swap_half)
    for pairs in (X_ONE, X_TWO, H_SWAP):
        squares = squares + lax.ppermute(squares, "tp", pairs)
    turns = turns_of(squares, width, positions)
    keep, turns = lax.optimization_barrier((keep, turns))
    keep_src = gather(across(keep))

    def sums(layer, src, which):
        return product(flags, scaled[layer], own, layer, src, which)

    came = [swapped(*round_x(*sums(layer, swap_src, 0))) for layer in range(LAYERS)]
    out = None
    for layer in range(LAYERS):
        out = close(layer, round_x(*sums(layer, keep_src, 1)), came[layer], turns[layer], out)
    return out


def solution(mesh):
    placed = (
        P("chain", "tp"),
        P("chain", "tp"),
        P("chain", None, "tp", None),
        P("chain", None, "tp"),
        P("chain"),
        P("chain"),
    )
    return jax.shard_map(
        shards, mesh=mesh, in_specs=placed, out_specs=P(None, "chain", "tp"), check_vma=False
    )
```

```python
import functools

import jax
import jax.numpy as jnp
from jax import lax
from jax.experimental import pallas as pl
from jax.experimental.pallas import tpu as pltpu
from jax.sharding import PartitionSpec as P

HD = 128
WIDE = 2 * HD
LAYERS = 2
NY, NX, NZ = 4, 4, 4
VMEM_LARGE, VMEM_SMALL = 52 << 20, 20 << 20
LOW = jnp.bfloat16
COLUMNS = LAYERS


def tp_pairs(step):
    pairs = []
    for h in range(2):
        for x in range(NX):
            h2, x2 = step(h, x)
            pairs.append((h * NX + x, (h2 % 2) * NX + x2 % NX))
    return pairs


def chain_pairs(step):
    pairs = []
    for z in range(NZ):
        for y in range(NY):
            for c in range(2):
                to = step(z, y, c)
                if to is not None:
                    z2, y2, c2 = to
                    pairs.append(((z * NY + y) * 2 + c, (z2 * NY + y2 % NY) * 2 + c2))
    return pairs


X_NEXT = tp_pairs(lambda h, x: (h, x + 1))
X_LAST = tp_pairs(lambda h, x: (h, x - 1))
X_ONE = tp_pairs(lambda h, x: (h, x ^ 1))
X_TWO = tp_pairs(lambda h, x: (h, x ^ 2))
H_SWAP = tp_pairs(lambda h, x: (h + 1, x))
Z_FAR = chain_pairs(lambda z, y, c: (2, y, 0) if (z, c) == (0, 0) else None)
Z_NEAR = chain_pairs(lambda z, y, c: (z + 1, y, 0) if z in (0, 2) and c == 0 else None)
CORE = chain_pairs(lambda z, y, c: (z, y, 1) if c == 0 else None)
ROWS = [[z * NY * 2 + k for k in range(NY * 2)] for z in range(NZ)]


def from_source(k):
    return chain_pairs(lambda z, y, c: (0, k, 0) if (z, y, c) == (0, 0, 0) else None)


def after(value, *earlier):
    return lax.optimization_barrier((value, earlier))[0]


def place():
    tp, chain = lax.axis_index("tp"), lax.axis_index("chain")
    return tp // NX, tp % NX, chain // (2 * NY), chain // 2 % NY, chain % 2


def dot(a, b):
    return jnp.dot(a, b, preferred_element_type=jnp.float32)


def pieces_kernel(flags, w_ref, g_ref, *refs):
    out_refs, (raw, near, sems) = refs[:NY], refs[NY:]
    depth, wide = out_refs[0].shape[1:]
    column = pl.multiple_of(flags[0] * wide, wide)

    def read(y):
        rows = pl.ds(y * depth, depth)
        return pltpu.make_async_copy(w_ref.at[0, :, rows, pl.ds(column, wide)], raw.at[y], sems.at[y])

    order = (2, 1, 3, 0)
    gain_copy = pltpu.make_async_copy(g_ref, near, sems.at[NY])
    gain_copy.start()
    for y in order:
        read(y).start()
    gain_copy.wait()
    gains = []
    for layer in range(LAYERS):
        row = near[0, layer:layer + 1, :].astype(jnp.float32)
        gains.append(jnp.broadcast_to(row, (HD, row.shape[1])).T)
    for y in order:
        read(y).wait()
        for layer in range(LAYERS):
            gain = gains[layer][y * depth:(y + 1) * depth]
            for at in range(0, wide, HD):
                out_refs[y][layer, :, at:at + HD] = (raw[y, layer, :, at:at + HD].astype(jnp.float32) * gain).astype(LOW)


def pieces(weights, gains, row):
    depth, wide = weights.shape[2] // NY, weights.shape[3] // 2
    vmem = pl.BlockSpec(memory_space=pltpu.VMEM)
    shape = (LAYERS, depth, wide)
    return pl.pallas_call(
        pieces_kernel,
        out_shape=tuple(jax.ShapeDtypeStruct(shape, LOW) for _ in range(NY)),
        in_specs=[pl.BlockSpec(memory_space=pltpu.SMEM), pl.BlockSpec(memory_space=pltpu.HBM), pl.BlockSpec(memory_space=pltpu.HBM)],
        out_specs=tuple(vmem for _ in range(NY)),
        scratch_shapes=[pltpu.VMEM((NY, *shape), LOW), pltpu.VMEM(gains.shape, LOW), pltpu.SemaphoreType.DMA((NY + 1,))],
        compiler_params=pltpu.CompilerParams(vmem_limit_bytes=VMEM_LARGE),
        cost_estimate=pl.CostEstimate(
            flops=LAYERS * NY * depth * wide, bytes_accessed=4 * LAYERS * NY * depth * wide, transcendentals=0
        ),
    )(row.astype(jnp.int32).reshape(1), weights, gains)


def scatter(parts):
    y = place()[3]
    got = {k: lax.ppermute(parts[k], "chain", from_source(k)) for k in (2, 1, 3)}
    return jnp.where(y == 0, parts[0], jnp.where(y == 1, got[1], jnp.where(y == 2, got[2], got[3])))


def down(first):
    z = place()[2]
    far = lax.ppermute(first, "chain", Z_FAR)
    second = jnp.where(z == 2, far, first)
    near = lax.ppermute(second, "chain", Z_NEAR)
    return jnp.where((z == 1) | (z == 3), near, second)


def across(mine):
    cut = mine.shape[1] // 2
    other = lax.ppermute(mine[:, cut:], "chain", CORE)
    return jnp.where(place()[4] == 0, mine[:, :cut], other)


def gather(half):
    return lax.all_gather(half, "chain", axis_index_groups=ROWS, axis=0)


def product_kernel(layer, first, flags, x_ref, own_ref, src_ref, plus_ref, minus_ref, keep_ref, blocks, sems):
    held = flags[layer] > 0
    cut = x_ref.shape[0] // 2

    def goal_of(j):
        return blocks.at[j // 2, :, :, pl.ds(j % 2 * WIDE, WIDE)]

    for j in range(NX):
        head = flags[first + j]

        @pl.when(held)
        def _():
            column = pl.ds(pl.multiple_of(head * WIDE, WIDE), WIDE)
            pltpu.make_async_copy(own_ref.at[0, layer, :, :, column], goal_of(j), sems.at[j]).start()

        @pl.when(jnp.logical_not(held))
        def _():
            column = pl.ds(pl.multiple_of(head % NX * WIDE, WIDE), WIDE)
            pltpu.make_async_copy(src_ref.at[:, layer, :, column], goal_of(j), sems.at[j]).start()

    low, high = slice(0, cut), slice(cut, 2 * cut)
    goals = (
        ((plus_ref, 0, low), (minus_ref, 0, high)),
        ((plus_ref, 1, high), (keep_ref, 0, low)),
        ((minus_ref, 1, low), (keep_ref, 1, high)),
        ((keep_ref, 2, low), (keep_ref, 3, high)),
    )
    for pair in range(NX // 2):
        for j in (2 * pair, 2 * pair + 1):
            pltpu.make_async_copy(src_ref.at[:, layer, :, pl.ds(0, WIDE)], goal_of(j), sems.at[j]).wait()
        block = blocks[pair].reshape(-1, 2 * WIDE)
        for rows in (low, high):
            total = dot(x_ref[rows, :], block).astype(LOW)
            for k in range(2):
                for ref, slot, where in goals[2 * pair + k]:
                    if where == rows:
                        ref[slot] = total[:, k * WIDE:(k + 1) * WIDE]


def product(flags, x, own, layer, src, which):
    tokens, depth = x.shape
    shapes = [(2, tokens // 2, WIDE), (2, tokens // 2, WIDE), (4, tokens // 2, WIDE)]
    vmem, hbm = pl.BlockSpec(memory_space=pltpu.VMEM), pl.BlockSpec(memory_space=pltpu.HBM)
    return pl.pallas_call(
        functools.partial(product_kernel, layer, COLUMNS + which * NX),
        out_shape=tuple(jax.ShapeDtypeStruct(shape, LOW) for shape in shapes),
        in_specs=[pl.BlockSpec(memory_space=pltpu.SMEM), vmem, hbm, hbm],
        out_specs=(vmem, vmem, vmem),
        scratch_shapes=[
            pltpu.VMEM((NX // 2, 2 * NY, depth // (2 * NY), 2 * WIDE), LOW),
            pltpu.SemaphoreType.DMA((NX,)),
        ],
        compiler_params=pltpu.CompilerParams(vmem_limit_bytes=VMEM_LARGE),
        cost_estimate=pl.CostEstimate(
            flops=2 * tokens * depth * WIDE * NX,
            bytes_accessed=2 * (tokens * depth + NX * WIDE * (depth + tokens)),
            transcendentals=0,
        ),
    )(flags, x, own, src)


def add(*terms):
    return sum(t.astype(jnp.float32) for t in terms)


def round_x(plus, minus, keep):
    plus1 = lax.ppermute(plus, "tp", X_NEXT)
    minus1 = lax.ppermute(minus, "tp", X_LAST)
    plus2 = lax.ppermute(add(keep[0], plus1[0]).astype(LOW), "tp", X_NEXT)
    minus2 = lax.ppermute(add(keep[1], minus1[0]).astype(LOW), "tp", X_LAST)
    return keep, plus1, minus1, plus2, minus2


def swapped(keep, plus1, minus1, plus2, minus2):
    low = add(keep[2], plus2, minus1[1])
    high = add(keep[3], minus2, plus1[1])
    return lax.ppermute(jnp.stack([low, high]).astype(LOW), "tp", H_SWAP)


def close_kernel(keep_ref, plus1, minus1, plus2, minus2, came_ref, cos_ref, sin_ref, scale_ref, *refs):
    out_ref = refs[-1]
    cut = keep_ref.shape[1]
    for i, (one, two) in enumerate(((minus1, plus2), (plus1, minus2))):
        rows = slice(i * cut, (i + 1) * cut)
        total = add(keep_ref[2 + i], one[1], two[...], came_ref[i])
        key = total[:, :HD]
        turned = key * cos_ref[rows, :] + pltpu.roll(key, HD // 2, 1) * sin_ref[rows, :]
        out_ref[rows, :HD] = turned.astype(LOW)
        out_ref[rows, HD:] = (total[:, HD:] * scale_ref[rows, :]).astype(LOW)


def close(layer, terms, came, turns, out):
    tokens = turns[0].shape[0]
    args = [*terms, came, *turns]
    in_specs = [pl.BlockSpec(memory_space=pltpu.VMEM) for _ in args]
    aliases = {}
    if out is not None:
        aliases = {len(args): 0}
        args.append(out)
        in_specs.append(pl.BlockSpec(memory_space=pl.ANY))
    return pl.pallas_call(
        close_kernel,
        out_shape=jax.ShapeDtypeStruct((LAYERS, tokens, WIDE), LOW),
        grid=(1,),
        in_specs=in_specs,
        out_specs=pl.BlockSpec((None, tokens, WIDE), lambda i: (layer, 0, 0)),
        input_output_aliases=aliases,
        compiler_params=pltpu.CompilerParams(vmem_limit_bytes=VMEM_SMALL),
        cost_estimate=pl.CostEstimate(flops=8 * tokens * WIDE, bytes_accessed=16 * tokens * WIDE, transcendentals=0),
    )(*args)


def flags_of(loaded_layers):
    h, x = place()[:2]
    flags = [(loaded_layers[0] > layer).astype(jnp.int32) for layer in range(LAYERS)]
    flags += [row * NX + (x + d) % NX for row in (1 - h, h) for d in (2, 1, 3, 0)]
    return jnp.stack(flags).astype(jnp.int32)


def turns_of(squares, width, positions):
    scale = lax.rsqrt(squares / width + 1e-05)[:, :, None]
    half = HD // 2
    freq = 500000.0 ** (-2.0 * jnp.arange(half, dtype=jnp.float32) / HD)
    angle = positions.astype(jnp.float32)[:, None] * freq[None, :]
    cosine, sine = jnp.cos(angle), jnp.sin(angle)
    cosine, sine = jnp.concatenate([cosine, cosine], 1), jnp.concatenate([-sine, sine], 1)
    return [(cosine * s, sine * s, jnp.broadcast_to(s, cosine.shape)) for s in scale]


def shards(hidden_first, hidden_second, weight_buffer, gain_buffer, loaded_layers, positions):
    inputs = (hidden_first, hidden_second)
    width = hidden_first.shape[1] * lax.axis_size("tp")
    flags = flags_of(loaded_layers)
    h = place()[0]
    own = weight_buffer.reshape(1, LAYERS, 2 * NY, -1, weight_buffer.shape[3])
    swap = scatter(pieces(weight_buffer, gain_buffer, 1 - h))
    keep_parts = pieces(weight_buffer, gain_buffer, h)
    wide = [v.astype(jnp.float32) for v in inputs]
    squares = jnp.stack([jnp.sum(jnp.square(v), axis=1) for v in wide])
    scaled = [
        jnp.where(loaded_layers[0] > layer, (v * gain_buffer[0, layer][None, :].astype(jnp.float32)).astype(LOW), inputs[layer])
        for layer, v in enumerate(wide)
    ]

    swap, keep_parts, squares, scaled = lax.optimization_barrier((swap, keep_parts, squares, scaled))
    keep = scatter(keep_parts)
    swap = down(swap)
    swap, keep = lax.optimization_barrier((swap, keep))
    swap_half = across(swap)
    swap_src = gather(swap_half)
    z = place()[2]
    far = lax.ppermute(after(keep, swap_half), "chain", Z_FAR)
    squares = after(squares, swap_half)
    squares = squares + lax.ppermute(squares, "tp", H_SWAP)
    far, squares = lax.optimization_barrier((far, squares))
    second = jnp.where(z == 2, far, keep)
    near = lax.ppermute(second, "chain", Z_NEAR)
    for pairs in (X_ONE, X_TWO):
        squares = squares + lax.ppermute(squares, "tp", pairs)
    turns = turns_of(squares, width, positions)
    near, turns = lax.optimization_barrier((near, turns))
    keep_src = gather(across(jnp.where((z == 1) | (z == 3), near, second)))

    def sums(layer, src, which):
        return product(flags, scaled[layer], own, layer, src, which)

    came = [swapped(*round_x(*sums(layer, swap_src, 0))) for layer in range(LAYERS)]
    out = None
    for layer in range(LAYERS):
        out = close(layer, round_x(*sums(layer, keep_src, 1)), came[layer], turns[layer], out)
    return out


def solution(mesh):
    placed = (
        P("chain", "tp"),
        P("chain", "tp"),
        P("chain", None, "tp", None),
        P("chain", None, "tp"),
        P("chain"),
        P("chain"),
    )
    return jax.shard_map(
        shards, mesh=mesh, in_specs=placed, out_specs=P(None, "chain", "tp"), check_vma=False
    )
```

```python
import functools

import jax
import jax.numpy as jnp
from jax import lax
from jax.experimental import pallas as pl
from jax.experimental.pallas import tpu as pltpu
from jax.sharding import PartitionSpec as P

HD = 128
WIDE = 2 * HD
LAYERS = 2
NY, NX, NZ = 4, 4, 4
VMEM_LARGE, VMEM_SMALL = 52 << 20, 20 << 20
LOW = jnp.bfloat16
COLUMNS = LAYERS


def tp_pairs(step):
    pairs = []
    for h in range(2):
        for x in range(NX):
            h2, x2 = step(h, x)
            pairs.append((h * NX + x, (h2 % 2) * NX + x2 % NX))
    return pairs


def chain_pairs(step):
    pairs = []
    for z in range(NZ):
        for y in range(NY):
            for c in range(2):
                to = step(z, y, c)
                if to is not None:
                    z2, y2, c2 = to
                    pairs.append(((z * NY + y) * 2 + c, (z2 * NY + y2 % NY) * 2 + c2))
    return pairs


X_NEXT = tp_pairs(lambda h, x: (h, x + 1))
X_LAST = tp_pairs(lambda h, x: (h, x - 1))
X_ONE = tp_pairs(lambda h, x: (h, x ^ 1))
X_TWO = tp_pairs(lambda h, x: (h, x ^ 2))
H_SWAP = tp_pairs(lambda h, x: (h + 1, x))
Z_FAR = chain_pairs(lambda z, y, c: (2, y, 0) if (z, c) == (0, 0) else None)
Z_NEAR = chain_pairs(lambda z, y, c: (z + 1, y, 0) if z in (0, 2) and c == 0 else None)
CORE = chain_pairs(lambda z, y, c: (z, y, 1) if c == 0 else None)
ROWS = [[z * NY * 2 + k for k in range(NY * 2)] for z in range(NZ)]


def from_source(k):
    return chain_pairs(lambda z, y, c: (0, k, 0) if (z, y, c) == (0, 0, 0) else None)


def after(value, *earlier):
    return lax.optimization_barrier((value, earlier))[0]


def place():
    tp, chain = lax.axis_index("tp"), lax.axis_index("chain")
    return tp // NX, tp % NX, chain // (2 * NY), chain // 2 % NY, chain % 2


def dot(a, b):
    return jnp.dot(a, b, preferred_element_type=jnp.float32)


def pieces_kernel(order, flags, w_ref, g_ref, *refs):
    *out_refs, raw, near, sems = refs
    depth, wide = out_refs[0].shape[1:]
    column = pl.multiple_of(flags[0] * wide, wide)

    def read(y):
        rows = pl.ds(y * depth, depth)
        k = order.index(y)
        return pltpu.make_async_copy(w_ref.at[0, :, rows, pl.ds(column, wide)], raw.at[k], sems.at[k])

    gain_copy = pltpu.make_async_copy(g_ref, near, sems.at[len(order)])
    gain_copy.start()
    for y in order:
        read(y).start()
    gain_copy.wait()
    gains = []
    for layer in range(LAYERS):
        row = near[0, layer:layer + 1, :].astype(jnp.float32)
        gains.append(jnp.broadcast_to(row, (HD, row.shape[1])).T)
    for k, y in enumerate(order):
        read(y).wait()
        for layer in range(LAYERS):
            gain = gains[layer][y * depth:(y + 1) * depth]
            for at in range(0, wide, HD):
                out_refs[k][layer, :, at:at + HD] = (raw[k, layer, :, at:at + HD].astype(jnp.float32) * gain).astype(LOW)


def pieces(weights, gains, row, order):
    depth, wide = weights.shape[2] // NY, weights.shape[3] // 2
    vmem = pl.BlockSpec(memory_space=pltpu.VMEM)
    shape = (LAYERS, depth, wide)
    parts = pl.pallas_call(
        functools.partial(pieces_kernel, order),
        out_shape=tuple(jax.ShapeDtypeStruct(shape, LOW) for _ in order),
        in_specs=[pl.BlockSpec(memory_space=pltpu.SMEM), pl.BlockSpec(memory_space=pltpu.HBM), pl.BlockSpec(memory_space=pltpu.HBM)],
        out_specs=tuple(vmem for _ in order),
        scratch_shapes=[pltpu.VMEM((len(order), *shape), LOW), pltpu.VMEM(gains.shape, LOW), pltpu.SemaphoreType.DMA((len(order) + 1,))],
        compiler_params=pltpu.CompilerParams(vmem_limit_bytes=VMEM_LARGE),
        cost_estimate=pl.CostEstimate(
            flops=LAYERS * len(order) * depth * wide, bytes_accessed=4 * LAYERS * len(order) * depth * wide, transcendentals=0
        ),
    )(row.astype(jnp.int32).reshape(1), weights, gains)
    return dict(zip(order, parts))


def scatter(parts):
    y = place()[3]
    got = {k: lax.ppermute(parts[k], "chain", from_source(k)) for k in (2, 1, 3)}
    return jnp.where(y == 0, parts[0], jnp.where(y == 1, got[1], jnp.where(y == 2, got[2], got[3])))


def down(first):
    z = place()[2]
    far = lax.ppermute(first, "chain", Z_FAR)
    second = jnp.where(z == 2, far, first)
    near = lax.ppermute(second, "chain", Z_NEAR)
    return jnp.where((z == 1) | (z == 3), near, second)


def across(mine):
    cut = mine.shape[1] // 2
    other = lax.ppermute(mine[:, cut:], "chain", CORE)
    return jnp.where(place()[4] == 0, mine[:, :cut], other)


def gather(half):
    return lax.all_gather(half, "chain", axis_index_groups=ROWS, axis=0)


def product_kernel(layer, first, flags, x_ref, own_ref, src_ref, plus_ref, minus_ref, keep_ref, blocks, sems):
    held = flags[layer] > 0
    cut = x_ref.shape[0] // 2

    def goal_of(j):
        return blocks.at[j // 2, :, :, pl.ds(j % 2 * WIDE, WIDE)]

    for j in range(NX):
        head = flags[first + j]

        @pl.when(held)
        def _():
            column = pl.ds(pl.multiple_of(head * WIDE, WIDE), WIDE)
            pltpu.make_async_copy(own_ref.at[0, layer, :, :, column], goal_of(j), sems.at[j]).start()

        @pl.when(jnp.logical_not(held))
        def _():
            column = pl.ds(pl.multiple_of(head % NX * WIDE, WIDE), WIDE)
            pltpu.make_async_copy(src_ref.at[:, layer, :, column], goal_of(j), sems.at[j]).start()

    low, high = slice(0, cut), slice(cut, 2 * cut)
    goals = (
        ((plus_ref, 0, low), (minus_ref, 0, high)),
        ((plus_ref, 1, high), (keep_ref, 0, low)),
        ((minus_ref, 1, low), (keep_ref, 1, high)),
        ((keep_ref, 2, low), (keep_ref, 3, high)),
    )
    for pair in range(NX // 2):
        for j in (2 * pair, 2 * pair + 1):
            pltpu.make_async_copy(src_ref.at[:, layer, :, pl.ds(0, WIDE)], goal_of(j), sems.at[j]).wait()
        block = blocks[pair].reshape(-1, 2 * WIDE)
        for rows in (low, high):
            total = dot(x_ref[rows, :], block).astype(LOW)
            for k in range(2):
                for ref, slot, where in goals[2 * pair + k]:
                    if where == rows:
                        ref[slot] = total[:, k * WIDE:(k + 1) * WIDE]


def product(flags, x, own, layer, src, which):
    tokens, depth = x.shape
    shapes = [(2, tokens // 2, WIDE), (2, tokens // 2, WIDE), (4, tokens // 2, WIDE)]
    vmem, hbm = pl.BlockSpec(memory_space=pltpu.VMEM), pl.BlockSpec(memory_space=pltpu.HBM)
    return pl.pallas_call(
        functools.partial(product_kernel, layer, COLUMNS + which * NX),
        out_shape=tuple(jax.ShapeDtypeStruct(shape, LOW) for shape in shapes),
        in_specs=[pl.BlockSpec(memory_space=pltpu.SMEM), vmem, hbm, hbm],
        out_specs=(vmem, vmem, vmem),
        scratch_shapes=[
            pltpu.VMEM((NX // 2, 2 * NY, depth // (2 * NY), 2 * WIDE), LOW),
            pltpu.SemaphoreType.DMA((NX,)),
        ],
        compiler_params=pltpu.CompilerParams(vmem_limit_bytes=VMEM_LARGE),
        cost_estimate=pl.CostEstimate(
            flops=2 * tokens * depth * WIDE * NX,
            bytes_accessed=2 * (tokens * depth + NX * WIDE * (depth + tokens)),
            transcendentals=0,
        ),
    )(flags, x, own, src)


def add(*terms):
    return sum(t.astype(jnp.float32) for t in terms)


def round_x(plus, minus, keep):
    plus1 = lax.ppermute(plus, "tp", X_NEXT)
    minus1 = lax.ppermute(minus, "tp", X_LAST)
    plus2 = lax.ppermute(add(keep[0], plus1[0]).astype(LOW), "tp", X_NEXT)
    minus2 = lax.ppermute(add(keep[1], minus1[0]).astype(LOW), "tp", X_LAST)
    return keep, plus1, minus1, plus2, minus2


def swapped(keep, plus1, minus1, plus2, minus2):
    low = add(keep[2], plus2, minus1[1])
    high = add(keep[3], minus2, plus1[1])
    return lax.ppermute(jnp.stack([low, high]).astype(LOW), "tp", H_SWAP)


def close_kernel(keep_ref, plus1, minus1, plus2, minus2, came_ref, cos_ref, sin_ref, scale_ref, *refs):
    out_ref = refs[-1]
    cut = keep_ref.shape[1]
    for i, (one, two) in enumerate(((minus1, plus2), (plus1, minus2))):
        rows = slice(i * cut, (i + 1) * cut)
        total = add(keep_ref[2 + i], one[1], two[...], came_ref[i])
        key = total[:, :HD]
        turned = key * cos_ref[rows, :] + pltpu.roll(key, HD // 2, 1) * sin_ref[rows, :]
        out_ref[rows, :HD] = turned.astype(LOW)
        out_ref[rows, HD:] = (total[:, HD:] * scale_ref[rows, :]).astype(LOW)


def close(layer, terms, came, turns, out):
    tokens = turns[0].shape[0]
    args = [*terms, came, *turns]
    in_specs = [pl.BlockSpec(memory_space=pltpu.VMEM) for _ in args]
    aliases = {}
    if out is not None:
        aliases = {len(args): 0}
        args.append(out)
        in_specs.append(pl.BlockSpec(memory_space=pl.ANY))
    return pl.pallas_call(
        close_kernel,
        out_shape=jax.ShapeDtypeStruct((LAYERS, tokens, WIDE), LOW),
        grid=(1,),
        in_specs=in_specs,
        out_specs=pl.BlockSpec((None, tokens, WIDE), lambda i: (layer, 0, 0)),
        input_output_aliases=aliases,
        compiler_params=pltpu.CompilerParams(vmem_limit_bytes=VMEM_SMALL),
        cost_estimate=pl.CostEstimate(flops=8 * tokens * WIDE, bytes_accessed=16 * tokens * WIDE, transcendentals=0),
    )(*args)


def flags_of(loaded_layers):
    h, x = place()[:2]
    flags = [(loaded_layers[0] > layer).astype(jnp.int32) for layer in range(LAYERS)]
    flags += [row * NX + (x + d) % NX for row in (1 - h, h) for d in (2, 1, 3, 0)]
    return jnp.stack(flags).astype(jnp.int32)


def turns_of(squares, width, positions):
    scale = lax.rsqrt(squares / width + 1e-05)[:, :, None]
    half = HD // 2
    freq = 500000.0 ** (-2.0 * jnp.arange(half, dtype=jnp.float32) / HD)
    angle = positions.astype(jnp.float32)[:, None] * freq[None, :]
    cosine, sine = jnp.cos(angle), jnp.sin(angle)
    cosine, sine = jnp.concatenate([cosine, cosine], 1), jnp.concatenate([-sine, sine], 1)
    return [(cosine * s, sine * s, jnp.broadcast_to(s, cosine.shape)) for s in scale]


def shards(hidden_first, hidden_second, weight_buffer, gain_buffer, loaded_layers, positions):
    inputs = (hidden_first, hidden_second)
    width = hidden_first.shape[1] * lax.axis_size("tp")
    flags = flags_of(loaded_layers)
    h = place()[0]
    own = weight_buffer.reshape(1, LAYERS, 2 * NY, -1, weight_buffer.shape[3])
    soon = pieces(weight_buffer, gain_buffer, 1 - h, (2,))
    swap = scatter(soon | pieces(weight_buffer, gain_buffer, 1 - h, (1, 3, 0)))
    keep_parts = pieces(weight_buffer, gain_buffer, h, (2, 1, 3, 0))
    wide = [v.astype(jnp.float32) for v in inputs]
    squares = jnp.stack([jnp.sum(jnp.square(v), axis=1) for v in wide])
    scaled = [
        jnp.where(loaded_layers[0] > layer, (v * gain_buffer[0, layer][None, :].astype(jnp.float32)).astype(LOW), inputs[layer])
        for layer, v in enumerate(wide)
    ]

    swap, keep_parts, squares, scaled = lax.optimization_barrier((swap, keep_parts, squares, scaled))
    keep = scatter(keep_parts)
    swap = down(swap)
    swap, keep = lax.optimization_barrier((swap, keep))
    swap_half = across(swap)
    swap_src = gather(swap_half)
    z = place()[2]
    far = lax.ppermute(after(keep, swap_half), "chain", Z_FAR)
    squares = after(squares, swap_half)
    squares = squares + lax.ppermute(squares, "tp", H_SWAP)
    far, squares = lax.optimization_barrier((far, squares))
    second = jnp.where(z == 2, far, keep)
    near = lax.ppermute(second, "chain", Z_NEAR)
    for pairs in (X_ONE, X_TWO):
        squares = squares + lax.ppermute(squares, "tp", pairs)
    turns = turns_of(squares, width, positions)
    near, turns = lax.optimization_barrier((near, turns))
    keep_src = gather(across(jnp.where((z == 1) | (z == 3), near, second)))

    def sums(layer, src, which):
        return product(flags, scaled[layer], own, layer, src, which)

    came = [swapped(*round_x(*sums(layer, swap_src, 0))) for layer in range(LAYERS)]
    out = None
    for layer in range(LAYERS):
        out = close(layer, round_x(*sums(layer, keep_src, 1)), came[layer], turns[layer], out)
    return out


def solution(mesh):
    placed = (
        P("chain", "tp"),
        P("chain", "tp"),
        P("chain", None, "tp", None),
        P("chain", None, "tp"),
        P("chain"),
        P("chain"),
    )
    return jax.shard_map(
        shards, mesh=mesh, in_specs=placed, out_specs=P(None, "chain", "tp"), check_vma=False
    )
```
